32 devices in a mesh: dp: 4 (over x, core), tensor: 8 (over z, y).
Axes of the slice: x: 2, y: 2, z: 4, core: 2. Of those that a mesh axis runs over, the one named last changes fastest.
Arguments:
- tokens: bfloat16 [2, 12288, 1024], P(None, ('dp', 'tensor')), may hold values from -6 to 6
- segment_ids: int32 [2, 4, 3072], P(None, 'dp'), may hold values from 0 to 3, never falling along the last dimension, each value on 1 to 1370 neighbouring positions
- out_grad: bfloat16 [2, 12288, 1024], P(None, ('dp', 'tensor')), may hold values from -6 to 6
- norm1_gain: bfloat16 [1024], P('dp'), may hold values from 0.25 to 1.75
- norm1_bias: bfloat16 [1024], P('dp'), may hold values from -3 to 3
- qkv_weight: bfloat16 [3, 1024, 1024], P(None, 'dp', 'tensor'), may hold values from -0.25 to 0.25
- qv_bias: bfloat16 [2, 1024], P(None, ('tensor', 'dp')), may hold values from -3 to 3
- proj_weight: bfloat16 [1024, 1024], P('tensor', 'dp'), may hold values from -1 to 1
- proj_bias: bfloat16 [1024], P('dp'), may hold values from -3 to 3
- scale1: bfloat16 [1024], P('dp'), may hold values from 0.25 to 1.75
- norm2_gain: bfloat16 [1024], P('dp'), may hold values from 0.25 to 1.75
- norm2_bias: bfloat16 [1024], P('dp'), may hold values from -3 to 3
- fc1_weight: bfloat16 [1024, 4096], P('dp', 'tensor'), may hold values from -0.1875 to 0.1875
- fc1_bias: bfloat16 [4096], P(('tensor', 'dp')), may hold values from -3 to 3
- fc2_weight: bfloat16 [4096, 1024], P('tensor', 'dp'), may hold values from -0.09375 to 0.09375
- fc2_bias: bfloat16 [1024], P('dp'), may hold values from -3 to 3
- scale2: bfloat16 [1024], P('dp'), may hold values from 0.25 to 1.75
Outputs:
- block_out: bfloat16 [2, 12288, 1024], P(None, ('dp', 'tensor'))
- tokens_grad: bfloat16 [2, 12288, 1024], P(None, ('dp', 'tensor'))
- grad_norm1_gain: float32 [1024], P('dp')
- grad_norm1_bias: float32 [1024], P('dp')
- grad_qkv_weight: float32 [3, 1024, 1024], P(None, 'dp', 'tensor')
- grad_qv_bias: float32 [2, 1024], P(None, ('tensor', 'dp'))
- grad_proj_weight: float32 [1024, 1024], P('tensor', 'dp')
- grad_proj_bias: float32 [1024], P('dp')
- grad_scale1: float32 [1024], P('dp')
- grad_norm2_gain: float32 [1024], P('dp')
- grad_norm2_bias: float32 [1024], P('dp')
- grad_fc1_weight: float32 [1024, 4096], P('dp', 'tensor')
- grad_fc1_bias: float32 [4096], P(('tensor', 'dp'))
- grad_fc2_weight: float32 [4096, 1024], P('tensor', 'dp')
- grad_fc2_bias: float32 [1024], P('dp')
- grad_scale2: float32 [1024], P('dp')
The draws below stay inside these ranges and needn't reach their ends.
Inputs may be any that keep to these rules, and one draw needn't show every extreme that they name: `segment_ids`: along each run the image number never falls; each image is a run of 1 to 1370 tokens, and some image has exactly 1370.
All inputs are finite; a program needn't handle non-finite values.
Results may differ from the reference program's by a relative error of at most 0.023.
Values may be sent and summed in bfloat16 or wider, within the bound.
A program may use at most 192 MiB of HBM per device.

```python
import math
from functools import partial
import jax
import jax.numpy as jnp
import numpy as np
from jax import lax

D = 1024
HEADS = 16
HEAD_DIM = 64
FF = 4096
IMG_MAX = 1370
TOK_DEV = 3072
MB = 2
MB_TOK = 12288
IMAGES = 4
N_DP = 4


def block_scale(rng, shape, split, smallest, top_value):
    level, own = 1.0, jax.random.fold_in(rng, 6)
    for position, parts in split:
        draws = jnp.exp(jax.random.uniform(jax.random.fold_in(own, position), (parts,), jnp.float32, smallest / len(split), top_value / len(split)))
        level = level * jnp.repeat(draws, shape[position] // parts).reshape([-1 if axis == position else 1 for axis in range(len(shape))])
    return level


def length_profile(amount, total, reach, lean):
    portions = [(1 << 20) // math.isqrt(standing ** lean) + 1 for standing in range(2, amount + 1)]
    surplus, holding = total - reach - (amount - 1), [1] * (amount - 1)
    while surplus > 0:
        candidates = [i for i in range(amount - 1) if holding[i] < reach]
        pool, left = sum([portions[i] for i in candidates]), surplus
        for i in candidates:
            more = min(reach - holding[i], max(1, left * portions[i] // pool), surplus)
            holding[i] = holding[i] + more
            surplus = surplus - more
    return np.array([reach] + holding)


def ragged(key, number_of, total, bound, slope):
    if number_of == 2:
        one = jax.random.randint(key, (), max(1, total - bound), min(bound, total - 1) + 1)
        return jnp.stack([one, total - one])
    lengths = jnp.asarray(length_profile(number_of, total, bound, slope), jnp.int32)
    twos = (number_of - 1) // 2
    donor, sink = lengths[1:1 + 2 * twos:2], lengths[2:2 + 2 * twos:2]
    margin = jnp.minimum(donor - 1, bound - sink)
    shifted = jax.random.randint(jax.random.fold_in(key, 1), (twos,), 0, 1 << 20) % (margin + 1)
    lengths = lengths.at[1:1 + 2 * twos:2].set(donor - shifted).at[2:2 + 2 * twos:2].set(sink + shifted)
    return lengths[jax.random.permutation(jax.random.fold_in(key, 2), number_of)]


def normal_values(stream_key, extent, scale, most, shards=(), held_as=jnp.bfloat16):
    level = block_scale(stream_key, extent, shards, -0.22, 0.18) if shards else 1.0
    values = jax.random.normal(stream_key, extent, jnp.float32) * scale * level
    return jnp.minimum(jnp.maximum(values, -most), most).astype(held_as)


def setup_inputs(seed: int = 0) -> dict:
    keys = jax.random.split(jax.random.key(seed), 18)
    tokens = normal_values(keys[0], (MB, MB_TOK, D), 1.0, 6.0, ((1, 32),))
    segment_ids = jax.vmap(lambda own: jnp.searchsorted(jnp.cumsum(ragged(own, IMAGES, TOK_DEV, IMG_MAX, 1)), jnp.arange(TOK_DEV), side="right"))(jax.random.split(keys[1], MB * N_DP)).reshape((MB, N_DP, TOK_DEV)).astype(jnp.int32)
    out_grad = normal_values(keys[2], (MB, MB_TOK, D), 1.0, 6.0, ((1, 32),))
    norm1_gain = jnp.clip(1.0 + 0.15 * jax.random.normal(keys[3], (D,), jnp.float32), 0.25, 1.75).astype(jnp.bfloat16)
    norm1_bias = normal_values(keys[4], (D,), 0.5, 3.0, ((0, 4),))
    qkv_weight = normal_values(keys[5], (3, D, D), (D // 2) ** -0.5, 0.25, ((1, 4), (2, 8)))
    qv_bias = normal_values(keys[6], (2, D), 0.5, 3.0, ((1, 32),))
    proj_weight = normal_values(keys[7], (D, D), (D // 32) ** -0.5, 1.0, ((0, 8), (1, 4)))
    proj_bias = normal_values(keys[8], (D,), 0.5, 3.0, ((0, 4),))
    scale1 = jnp.clip(1.0 + 0.15 * jax.random.normal(keys[9], (D,), jnp.float32), 0.25, 1.75).astype(jnp.bfloat16)
    norm2_gain = jnp.clip(1.0 + 0.15 * jax.random.normal(keys[10], (D,), jnp.float32), 0.25, 1.75).astype(jnp.bfloat16)
    norm2_bias = normal_values(keys[11], (D,), 0.5, 3.0, ((0, 4),))
    fc1_weight = normal_values(keys[12], (D, FF), D ** -0.5, 0.1875, ((0, 4), (1, 8)))
    fc1_bias = normal_values(keys[13], (FF,), 0.5, 3.0, ((0, 32),))
    fc2_weight = normal_values(keys[14], (FF, D), FF ** -0.5, 0.09375, ((0, 8), (1, 4)))
    fc2_bias = normal_values(keys[15], (D,), 0.5, 3.0, ((0, 4),))
    scale2 = jnp.clip(1.0 + 0.15 * jax.random.normal(keys[16], (D,), jnp.float32), 0.25, 1.75).astype(jnp.bfloat16)
    return dict(tokens=tokens, segment_ids=segment_ids, out_grad=out_grad, norm1_gain=norm1_gain, norm1_bias=norm1_bias, qkv_weight=qkv_weight, qv_bias=qv_bias, proj_weight=proj_weight, proj_bias=proj_bias, scale1=scale1, norm2_gain=norm2_gain, norm2_bias=norm2_bias, fc1_weight=fc1_weight, fc1_bias=fc1_bias, fc2_weight=fc2_weight, fc2_bias=fc2_bias, scale2=scale2)


norm_eps = 1e-06
mask_fill = -1e+30
highest = lax.Precision.HIGHEST

@jax.custom_vjp
def low(v):
    return lax.optimization_barrier(v.astype(jnp.bfloat16)).astype(jnp.float32)

@jax.custom_vjp
def low_back(v):
    return v

def low_keep(v):
    return (low(v), None)

def low_pass(kept, grad):
    return (grad,)

def back_keep(v):
    return (v, None)

def back_low(kept, grad):
    return (low(grad),)
low.defvjp(low_keep, low_pass)
low_back.defvjp(back_keep, back_low)

def layer_norm(values, scale_gain, shift_bias):
    center = values - lax.optimization_barrier(jnp.mean(values, axis=-1, keepdims=True))
    spread = lax.optimization_barrier(jnp.mean(center * center, axis=-1, keepdims=True))
    return center * lax.rsqrt(spread + norm_eps) * scale_gain + shift_bias

def matmul(left, right):
    return jnp.dot(left, right, precision=highest, preferred_element_type=jnp.float32)

def attention(queries, keys_all, values_all, image_ids):
    block_rows = min(512, TOK_DEV)
    run_shape = (N_DP, TOK_DEV, HEADS, HEAD_DIM)

    def one_run(run_inputs):
        run_queries, run_keys, run_values, run_ids = run_inputs

        def one_block(block_id):
            row_start = (block_id * block_rows).astype(jnp.int32)
            query_block = lax.dynamic_slice_in_dim(run_queries, row_start, block_rows, 0)
            query_ids = lax.dynamic_slice_in_dim(run_ids, row_start, block_rows, 0)
            same_image = query_ids[:, None] == run_ids[None, :]
            scores = low_back(jnp.einsum('qhd,khd->hqk', query_block, run_keys, precision=highest))
            scores = jnp.where(same_image[None], scores, mask_fill)
            weights_p = low(jax.nn.softmax(scores, axis=-1))
            return jnp.einsum('hqk,khd->qhd', weights_p, run_values, precision=highest)
        blocks = lax.map(jax.checkpoint(one_block), jnp.arange(TOK_DEV // block_rows, dtype=jnp.int32))
        return blocks.reshape(TOK_DEV, HEADS, HEAD_DIM)
    runs = lax.map(one_run, (queries.reshape(run_shape), keys_all.reshape(run_shape), values_all.reshape(run_shape), image_ids))
    return runs.reshape(N_DP * TOK_DEV, HEADS * HEAD_DIM)

def forward(params, rows_in, image_ids):
    norm1_gain, norm1_bias, qkv_weight, qv_bias, proj_weight, proj_bias, scale1, norm2_gain, norm2_bias, fc1_weight, fc1_bias, fc2_weight, fc2_bias, scale2 = params
    normed_one = low(layer_norm(rows_in, norm1_gain, norm1_bias))
    queries = low(low_back((matmul(normed_one, qkv_weight[0]) + qv_bias[0]) * 0.125))
    keys_all = low(low_back(matmul(normed_one, qkv_weight[1])))
    values_all = low(low_back(matmul(normed_one, qkv_weight[2]) + qv_bias[1]))
    attended = attention(queries, keys_all, values_all, image_ids)
    attended = low(low_back(attended))
    branch_one = low_back(matmul(attended, proj_weight) + proj_bias)
    middle = rows_in + scale1 * branch_one
    normed_two = low(layer_norm(middle, norm2_gain, norm2_bias))
    pre_act = low_back(matmul(normed_two, fc1_weight) + fc1_bias)
    activated = low(jax.nn.gelu(pre_act, approximate=False))
    branch_two = low_back(matmul(activated, fc2_weight) + fc2_bias)
    return middle + scale2 * branch_two

def reference(tokens, segment_ids, out_grad, norm1_gain, norm1_bias, qkv_weight, qv_bias, proj_weight, proj_bias, scale1, norm2_gain, norm2_bias, fc1_weight, fc1_bias, fc2_weight, fc2_bias, scale2):
    params = tuple((param_arr.astype(jnp.float32) for param_arr in (norm1_gain, norm1_bias, qkv_weight, qv_bias, proj_weight, proj_bias, scale1, norm2_gain, norm2_bias, fc1_weight, fc1_bias, fc2_weight, fc2_bias, scale2)))
    gradients = tuple((jnp.zeros_like(param_arr) for param_arr in params))
    outputs = []
    input_grads = []
    for micro in range(MB):
        rows_in = tokens[micro].astype(jnp.float32)
        result, pullback = jax.vjp(partial(forward, image_ids=segment_ids[micro]), params, rows_in)
        param_grads, rows_grad = pullback(out_grad[micro].astype(jnp.float32))
        gradients = jax.tree.map(jnp.add, gradients, param_grads)
        outputs.append(result.astype(jnp.bfloat16))
        input_grads.append(rows_grad.astype(jnp.bfloat16))
    return (jnp.stack(outputs), jnp.stack(input_grads), gradients[0], gradients[1], gradients[2], gradients[3], gradients[4], gradients[5], gradients[6], gradients[7], gradients[8], gradients[9], gradients[10], gradients[11], gradients[12], gradients[13])
```

```python
import jax
import jax.numpy as jnp
from jax import lax
from jax.experimental import pallas as pl
from jax.experimental.pallas import tpu as pltpu
from jax.sharding import PartitionSpec as P

HEAD_DIM = 64

norm_eps = 1e-06
mask_fill = -1e30
query_rows = 512
key_rows = 512
contract_rows = (((0,), (0,)), ((), ()))
contract_cols = (((1,), (1,)), ((), ()))
everywhere = ("dp", "tensor")


def dot_f32(left, right, dims=(((1,), (0,)), ((), ()))):
    return lax.dot_general(left, right, dims, preferred_element_type=jnp.float32)


def norm_parts(values):
    center = values - jnp.mean(values, axis=-1, keepdims=True)
    rate = lax.rsqrt(jnp.mean(center * center, axis=-1, keepdims=True) + norm_eps)
    return center * rate, rate


def norm_back(normed, rate, gain, grad):
    scaled = gain * grad
    average = jnp.mean(scaled, axis=-1, keepdims=True)
    along = jnp.mean(scaled * normed, axis=-1, keepdims=True)
    return rate * (scaled - average - normed * along)


def head_part(rows, head):
    lane = lax.broadcasted_iota(jnp.int32, rows.shape, 1)
    return jnp.where(lane // HEAD_DIM == head, rows, jnp.zeros_like(rows))


def forward_kernel(low_ref, high_ref, q_ref, k_ref, v_ref, idq_ref, idk_ref, out_ref, lse_ref):
    batch, block = pl.program_id(0), pl.program_id(1)
    queries = q_ref[0]
    heads = queries.shape[1] // HEAD_DIM
    rows = queries.shape[0]
    parts = [head_part(queries, head) for head in range(heads)]
    ids_query = idq_ref[0]

    def step(index, carry):
        start = pl.multiple_of(index * key_rows, key_rows)
        keys = k_ref[0, pl.ds(start, key_rows), :]
        values = v_ref[0, pl.ds(start, key_rows), :].T
        same = idk_ref[0, pl.ds(start, key_rows), :] == ids_query
        result = []
        for head in range(heads):
            top, total, acc = carry[head]
            scores = jnp.where(same, dot_f32(keys, parts[head], contract_cols), mask_fill)
            new_top = jnp.maximum(top, jnp.max(scores, axis=0, keepdims=True))
            expon = jnp.exp(scores - new_top)
            shrink = jnp.exp(top - new_top)
            total = shrink * total + jnp.sum(expon, axis=0, keepdims=True)
            mine = values[head * HEAD_DIM : (head + 1) * HEAD_DIM]
            acc = shrink * acc + dot_f32(mine, expon.astype(jnp.bfloat16))
            result.append((new_top, total, acc))
        return tuple(result)

    start_carry = tuple(
        (
            jnp.full((1, rows), mask_fill, jnp.float32),
            jnp.zeros((1, rows), jnp.float32),
            jnp.zeros((HEAD_DIM, rows), jnp.float32),
        )
        for _ in range(heads)
    )
    final = lax.fori_loop(low_ref[batch, block], high_ref[batch, block], step, start_carry)
    merged = jnp.concatenate([acc / total for _, total, acc in final], axis=0)
    out_ref[0] = merged.T.astype(out_ref.dtype)
    lse_ref[0, 0] = jnp.concatenate([top + jnp.log(total) for top, total, _ in final], axis=0)


def backward_kernel(
    low_ref, high_ref, q_ref, k_ref, v_ref, idq_ref, idk_ref, att_ref, d_att_ref, lse_ref,
    dq_ref, dk_ref, dv_ref, dk_sum, dv_sum,
):
    batch, block = pl.program_id(0), pl.program_id(1)

    @pl.when(block == 0)
    def _():
        dk_sum[...] = jnp.zeros_like(dk_sum)
        dv_sum[...] = jnp.zeros_like(dv_sum)

    queries, d_att = q_ref[0], d_att_ref[0]
    heads = queries.shape[1] // HEAD_DIM
    rows = queries.shape[0]
    parts = [head_part(queries, head) for head in range(heads)]
    d_parts = [head_part(d_att, head) for head in range(heads)]
    ids_query = idq_ref[0]
    products = (att_ref[0].astype(jnp.float32) * d_att.astype(jnp.float32)).T
    inner = [
        jnp.sum(products[head * HEAD_DIM : (head + 1) * HEAD_DIM], axis=0, keepdims=True)
        for head in range(heads)
    ]
    lse = lse_ref[0, 0]

    def step(index, carry):
        start = pl.multiple_of(index * key_rows, key_rows)
        here = pl.ds(start, key_rows)
        keys, values = k_ref[0, here, :], v_ref[0, here, :]
        keys_turned = keys.T
        same = idk_ref[0, here, :] == ids_query
        result = []
        d_value, d_key = dv_sum[here, :], dk_sum[here, :]
        for head in range(heads):
            scores = jnp.where(same, dot_f32(keys, parts[head], contract_cols), mask_fill)
            probs = jnp.exp(scores - lse[head : head + 1])
            d_probs = dot_f32(values, d_parts[head], contract_cols)
            d_scores = (probs * (d_probs - inner[head])).astype(jnp.bfloat16)
            d_value = d_value + dot_f32(probs.astype(jnp.bfloat16), d_parts[head])
            d_key = d_key + dot_f32(d_scores, parts[head])
            mine = keys_turned[head * HEAD_DIM : (head + 1) * HEAD_DIM]
            result.append(carry[head] + dot_f32(mine, d_scores))
        dv_sum[here, :] = d_value
        dk_sum[here, :] = d_key
        return tuple(result)

    empty = tuple(jnp.zeros((HEAD_DIM, rows), jnp.float32) for _ in range(heads))
    final = lax.fori_loop(low_ref[batch, block], high_ref[batch, block], step, empty)
    dq_ref[0] = (jnp.concatenate(final, axis=0).T * 0.125).astype(dq_ref.dtype)

    @pl.when(block == pl.num_programs(1) - 1)
    def _():
        dk_ref[0] = dk_sum[...].astype(dk_ref.dtype)
        dv_ref[0] = dv_sum[...].astype(dv_ref.dtype)


def attention_inputs(qkv):
    cols = qkv.shape[2] // 3
    if cols % 128 == 0:
        return qkv, qkv, qkv
    return qkv[..., :cols], qkv[..., cols : 2 * cols], qkv[..., 2 * cols :]


def attention_specs(tok_count, cols):
    spot_k, spot_v = (1, 2) if cols % 128 == 0 else (0, 0)
    q_spec = pl.BlockSpec((1, query_rows, cols), lambda b, i, *_: (b, i, 0))
    k_spec = pl.BlockSpec((1, tok_count, cols), lambda b, i, *_: (b, 0, spot_k))
    v_spec = pl.BlockSpec((1, tok_count, cols), lambda b, i, *_: (b, 0, spot_v))
    whole = pl.BlockSpec((1, tok_count, cols), lambda b, i, *_: (b, 0, 0))
    idq_spec = pl.BlockSpec((1, 1, query_rows), lambda b, i, *_: (b, 0, i))
    idk_spec = pl.BlockSpec((1, tok_count, 1), lambda b, i, *_: (b, 0, 0))
    lse_spec = pl.BlockSpec(
        (1, 1, cols // HEAD_DIM, query_rows), lambda b, i, *_: (b, i, 0, 0)
    )
    return q_spec, k_spec, v_spec, whole, idq_spec, idk_spec, lse_spec


def attention(qkv, bounds, ids_row, ids_col):
    batches, tok_count, cols3 = qkv.shape
    cols = cols3 // 3
    blocks = tok_count // query_rows
    q_spec, k_spec, v_spec, _, idq_spec, idk_spec, lse_spec = attention_specs(
        tok_count, cols
    )
    pairs = batches * tok_count * tok_count // 2
    return pl.pallas_call(
        forward_kernel,
        grid_spec=pltpu.PrefetchScalarGridSpec(
            num_scalar_prefetch=2,
            grid=(batches, blocks),
            in_specs=[q_spec, k_spec, v_spec, idq_spec, idk_spec],
            out_specs=[q_spec, lse_spec],
        ),
        out_shape=[
            jax.ShapeDtypeStruct((batches, tok_count, cols), jnp.bfloat16),
            jax.ShapeDtypeStruct(
                (batches, blocks, cols // HEAD_DIM, query_rows), jnp.float32
            ),
        ],
        compiler_params=pltpu.CompilerParams(vmem_limit_bytes=40 * 1024 * 1024),
        cost_estimate=pl.CostEstimate(
            flops=pairs * 16 * cols, bytes_accessed=2 * qkv.size, transcendentals=2 * pairs
        ),
    )(*bounds, *attention_inputs(qkv), ids_row, ids_col)


def attention_back(qkv, bounds, ids_row, ids_col, att, d_att, lse):
    batches, tok_count, cols3 = qkv.shape
    cols = cols3 // 3
    blocks = tok_count // query_rows
    q_spec, k_spec, v_spec, whole, idq_spec, idk_spec, lse_spec = attention_specs(
        tok_count, cols
    )
    pairs = batches * tok_count * tok_count // 2
    one = jax.ShapeDtypeStruct((batches, tok_count, cols), jnp.bfloat16)
    return pl.pallas_call(
        backward_kernel,
        grid_spec=pltpu.PrefetchScalarGridSpec(
            num_scalar_prefetch=2,
            grid=(batches, blocks),
            in_specs=[q_spec, k_spec, v_spec, idq_spec, idk_spec, q_spec, q_spec, lse_spec],
            out_specs=[q_spec, whole, whole],
            scratch_shapes=[
                pltpu.VMEM((tok_count, cols), jnp.float32),
                pltpu.VMEM((tok_count, cols), jnp.float32),
            ],
        ),
        out_shape=[one, one, one],
        compiler_params=pltpu.CompilerParams(vmem_limit_bytes=48 * 1024 * 1024),
        cost_estimate=pl.CostEstimate(
            flops=pairs * 40 * cols, bytes_accessed=4 * qkv.size, transcendentals=2 * pairs
        ),
    )(*bounds, *attention_inputs(qkv), ids_row, ids_col, att, d_att, lse)


def gather_matrix(shard):
    part = lax.all_gather(shard, "tensor", axis=1, tiled=True)
    return lax.all_gather(part, "dp", axis=0, tiled=True)


def scatter_matrix(grad):
    part = lax.psum_scatter(grad.astype(jnp.bfloat16), "dp", scatter_dimension=0, tiled=True)
    return lax.psum_scatter(part, "tensor", scatter_dimension=1, tiled=True).astype(jnp.float32)


def body(
    tokens,
    segment_ids,
    out_grad,
    norm1_gain,
    norm1_bias,
    qkv_weight,
    qv_bias,
    proj_weight,
    proj_bias,
    scale1,
    norm2_gain,
    norm2_bias,
    fc1_weight,
    fc1_bias,
    fc2_weight,
    fc2_bias,
    scale2,
):
    tensor_count = lax.axis_size("tensor")
    dp_count = lax.axis_size("dp")
    batches, rows_here, width = tokens.shape
    total_rows = batches * rows_here
    tok_count = rows_here * tensor_count
    cols_here = qkv_weight.shape[2]
    shard_rows = qkv_weight.shape[1]
    hidden = fc1_weight.shape[1] * tensor_count

    vectors = jnp.stack(
        [norm1_gain, norm1_bias, proj_bias, scale1, norm2_gain, norm2_bias, fc2_bias, scale2]
    )
    vecs = lax.all_gather(vectors, "dp", axis=1, tiled=True).astype(jnp.float32)
    short = qv_bias.shape[1]
    biases = jnp.concatenate([qv_bias.reshape(-1), fc1_bias])
    biases = lax.all_gather(biases, ("tensor", "dp"), axis=0, tiled=False).astype(jnp.float32)
    bias_q = biases[:, :short].reshape(tensor_count, 1, cols_here)
    bias_v = biases[:, short : 2 * short].reshape(tensor_count, 1, cols_here)
    bias_fc1 = biases[:, 2 * short :].reshape(hidden)
    bias_qkv = jnp.concatenate([bias_q, jnp.zeros_like(bias_q), bias_v], axis=1).reshape(-1)
    scale_qkv = jnp.concatenate(
        [jnp.full_like(bias_q, 0.125), jnp.ones_like(bias_q), jnp.ones_like(bias_q)], axis=1
    ).reshape(-1)

    w_qkv = gather_matrix(jnp.moveaxis(qkv_weight, 0, 1).reshape(shard_rows, 3 * cols_here))
    w_proj = gather_matrix(proj_weight.T)
    w_fc1 = gather_matrix(fc1_weight)
    w_fc2 = gather_matrix(fc2_weight.T)

    run_ids = segment_ids[:, 0]
    blocks = tok_count // query_rows
    first = run_ids.reshape(batches, blocks, query_rows)[:, :, :1]
    last = run_ids.reshape(batches, blocks, query_rows)[:, :, -1:]
    low = jnp.sum((run_ids[:, None, :] < first).astype(jnp.int32), axis=-1) // key_rows
    reach = jnp.sum((run_ids[:, None, :] <= last).astype(jnp.int32), axis=-1)
    bounds = (low, (reach + key_rows - 1) // key_rows)
    ids_row, ids_col = run_ids[:, None, :], run_ids[:, :, None]

    rows_in = tokens.reshape(total_rows, width).astype(jnp.float32)
    normed_one, rate_one = norm_parts(rows_in)
    normed_one_low = (normed_one * vecs[0] + vecs[1]).astype(jnp.bfloat16)
    projected = ((dot_f32(normed_one_low, w_qkv) + bias_qkv) * scale_qkv).astype(jnp.bfloat16)
    qkv = lax.all_to_all(
        projected.reshape(batches, rows_here, tensor_count * 3 * cols_here),
        "tensor", split_axis=2, concat_axis=1, tiled=True,
    )
    att_heads, lse = attention(qkv, bounds, ids_row, ids_col)
    attended = lax.all_to_all(
        att_heads, "tensor", split_axis=1, concat_axis=2, tiled=True
    ).reshape(total_rows, width)
    branch_one = dot_f32(attended, w_proj, contract_cols) + vecs[2]
    middle = rows_in + vecs[3] * branch_one
    normed_two, rate_two = norm_parts(middle)
    mlp_in = (normed_two * vecs[4] + vecs[5]).astype(jnp.bfloat16)
    pre_act = dot_f32(mlp_in, w_fc1) + bias_fc1
    spread = 0.5 * (1.0 + lax.erf(pre_act * 0.7071067811865476))
    activated = (pre_act * spread).astype(jnp.bfloat16)
    slope = spread + pre_act * jnp.exp(-0.5 * pre_act * pre_act) * 0.3989422804014327
    branch_two = dot_f32(activated, w_fc2, contract_cols) + vecs[6]
    block_out = (middle + vecs[7] * branch_two).astype(jnp.bfloat16)

    grad_top = out_grad.reshape(total_rows, width).astype(jnp.float32)
    d_scale2 = jnp.sum(grad_top * branch_two, axis=0)
    d_branch2 = (vecs[7] * grad_top).astype(jnp.bfloat16)
    d_fc2_bias = jnp.sum(d_branch2.astype(jnp.float32), axis=0)
    d_fc2 = dot_f32(d_branch2, activated, contract_rows)
    d_pre = (dot_f32(d_branch2, w_fc2) * slope).astype(jnp.bfloat16)
    d_fc1_bias = jnp.sum(d_pre.astype(jnp.float32), axis=0)
    d_fc1 = dot_f32(mlp_in, d_pre, contract_rows)
    d_normed_two = dot_f32(d_pre, w_fc1, contract_cols)
    d_gain2 = jnp.sum(d_normed_two * normed_two, axis=0)
    d_bias2 = jnp.sum(d_normed_two, axis=0)
    d_middle = grad_top + norm_back(normed_two, rate_two, vecs[4], d_normed_two)
    d_scale1 = jnp.sum(d_middle * branch_one, axis=0)
    d_branch1 = (vecs[3] * d_middle).astype(jnp.bfloat16)
    d_proj_bias = jnp.sum(d_branch1.astype(jnp.float32), axis=0)
    d_proj = dot_f32(d_branch1, attended, contract_rows)
    d_attended = dot_f32(d_branch1, w_proj).astype(jnp.bfloat16)
    d_att_heads = lax.all_to_all(
        d_attended.reshape(batches, rows_here, width),
        "tensor", split_axis=2, concat_axis=1, tiled=True,
    )
    shard_fc2 = scatter_matrix(d_fc2)
    shard_fc1 = scatter_matrix(d_fc1)
    shard_proj = scatter_matrix(d_proj)
    d_heads = jnp.concatenate(
        attention_back(qkv, bounds, ids_row, ids_col, att_heads, d_att_heads, lse), axis=2
    )
    d_qkv = lax.all_to_all(d_heads, "tensor", split_axis=1, concat_axis=2, tiled=True)
    d_qkv = d_qkv.reshape(total_rows, tensor_count * 3 * cols_here)
    shard_qkv = scatter_matrix(dot_f32(normed_one_low, d_qkv, contract_rows))
    d_bias_qkv = jnp.sum(d_qkv.astype(jnp.float32), axis=0)
    d_normed_one = dot_f32(d_qkv, w_qkv, contract_cols)
    d_gain1 = jnp.sum(d_normed_one * normed_one, axis=0)
    d_bias1 = jnp.sum(d_normed_one, axis=0)
    input_grad = d_middle + norm_back(normed_one, rate_one, vecs[0], d_normed_one)

    early = [d_proj_bias, d_scale1, d_gain2, d_bias2, d_fc2_bias, d_scale2]
    summed = lax.psum(
        jnp.concatenate([d_gain1, d_bias1] + early + [d_fc1_bias, d_bias_qkv]), everywhere
    )
    place_dp = lax.axis_index("dp")
    place = lax.axis_index("tensor") * dp_count + place_dp
    vec_sums = summed[: 8 * width].reshape(8, width)
    vec_sums = lax.dynamic_slice_in_dim(vec_sums, place_dp * shard_rows, shard_rows, 1)
    fc1_sums = summed[8 * width : 8 * width + hidden]
    grad_fc1_bias = lax.dynamic_slice_in_dim(
        fc1_sums, place * fc1_bias.shape[0], fc1_bias.shape[0], 0
    )
    qkv_sums = summed[8 * width + hidden :].reshape(tensor_count, 3, cols_here)
    qv_sums = jnp.stack([qkv_sums[:, 0].reshape(-1), qkv_sums[:, 2].reshape(-1)])
    grad_qv_bias = lax.dynamic_slice_in_dim(qv_sums, place * short, short, 1)
    shape = tokens.shape
    return (
        block_out.reshape(shape),
        input_grad.astype(jnp.bfloat16).reshape(shape),
        vec_sums[0],
        vec_sums[1],
        jnp.moveaxis(shard_qkv.reshape(shard_rows, 3, cols_here), 1, 0),
        grad_qv_bias,
        shard_proj.T,
        vec_sums[2],
        vec_sums[3],
        vec_sums[4],
        vec_sums[5],
        shard_fc1,
        grad_fc1_bias,
        shard_fc2.T,
        vec_sums[6],
        vec_sums[7],
    )


def solution(mesh):
    in_specs = (
        P(None, ("dp", "tensor"), None),
        P(None, "dp", None),
        P(None, ("dp", "tensor"), None),
        P("dp"),
        P("dp"),
        P(None, "dp", "tensor"),
        P(None, ("tensor", "dp")),
        P("tensor", "dp"),
        P("dp"),
        P("dp"),
        P("dp"),
        P("dp"),
        P("dp", "tensor"),
        P(("tensor", "dp")),
        P("tensor", "dp"),
        P("dp"),
        P("dp"),
    )
    out_specs = (
        P(None, ("dp", "tensor"), None),
        P(None, ("dp", "tensor"), None),
        P("dp"),
        P("dp"),
        P(None, "dp", "tensor"),
        P(None, ("tensor", "dp")),
        P("tensor", "dp"),
        P("dp"),
        P("dp"),
        P("dp"),
        P("dp"),
        P("dp", "tensor"),
        P(("tensor", "dp")),
        P("tensor", "dp"),
        P("dp"),
        P("dp"),
    )
    return jax.shard_map(body, mesh=mesh, in_specs=in_specs, out_specs=out_specs, check_vma=False)
```
